256 devices in a mesh: ffn: 16 (over z_lo, x), emb: 16 (over z_hi, y, core).
Axes of the slice: x: 4, y: 4, z: 8 (z_hi: 2, z_lo: 4; z = z_hi * 4 + z_lo), core: 2. Of those that a mesh axis runs over, the one named last changes fastest.
Arguments:
- tokens: bfloat16 [256, 4, 18432], P('ffn', None, 'emb')
- ln_gain: bfloat16 [18432], P('emb'), may hold values from 0.099609375 to 1.8984375
- w_gate: bfloat16 [18432, 12288], P('emb', 'ffn'), may hold values from -0.046875 to 0.046875
- w_up: bfloat16 [18432, 12288], P('emb', 'ffn'), may hold values from -0.046875 to 0.046875
- w_down: bfloat16 [12288, 18432], P('ffn', 'emb'), may hold values from -0.0546875 to 0.0546875
- w_query: bfloat16 [18432, 12288], P('emb', 'ffn'), may hold values from -0.1875 to 0.1875
- w_kv: bfloat16 [18432, 512], P('emb'), may hold values from -0.046875 to 0.046875
- w_out: bfloat16 [12288, 18432], P('ffn', 'emb'), may hold values from -0.0546875 to 0.0546875
- cache_keys: bfloat16 [256, 2048, 256], P(('ffn', 'emb'))
- cache_values: bfloat16 [256, 2048, 256], P(('ffn', 'emb')), may hold values from -6 to 6
- lengths: int32 [256], P(('ffn', 'emb')), may hold values from 1 to 2048, as said below
- positions: int32 [256], P(('ffn', 'emb')), may hold values from 0 to 8191
Outputs:
- block_out: bfloat16 [256, 4, 18432], P('ffn', None, 'emb')
The draws below stay inside these ranges and needn't reach their ends.
Inputs may be any that keep to these rules, and one draw needn't show every extreme that they name: `lengths`: some sequence has exactly 2048 valid slots.
All inputs are finite; a program needn't handle non-finite values.
Results may differ from the reference program's by a relative error of at most 0.023.
Values may be sent and summed in bfloat16 or wider, within the bound.
No kernel may reach another device: no remote copies, remote signals or barrier semaphores. Data moves between devices by JAX's collectives and lax.ppermute only.
A program may use at most 128 MiB of HBM per device.

```python
import jax
import jax.numpy as jnp
from jax import lax

D = 18432
HEADS = 48
HEAD_DIM = 256
FF = 12288
DRAFT = 4
CACHE = 2048
SEQS = 256


def draw_tokens(key, part):
    key = jax.random.fold_in(key, 11)
    first = jax.random.fold_in(key, 0)
    ramp = 0.5 + 1.5 * jnp.arange(D).astype(jnp.float32) / (D - 1)
    values = jnp.clip(jax.random.normal(first, (SEQS, DRAFT, D)), -5.0, 5.0) * ramp
    return values.astype(jnp.bfloat16)


def draw_cache_keys(key, part):
    key = jax.random.fold_in(key, 23)
    base = jnp.clip(jax.random.normal(key, (SEQS, CACHE, HEAD_DIM)), -5.0, 5.0)
    return base.astype(jnp.bfloat16)


def draw_lengths(key, part):
    key = jax.random.fold_in(key, 37)
    first, second = jax.random.split(key)
    values = jax.random.randint(first, (SEQS,), 1, CACHE + 1)
    chosen = jax.random.randint(second, (), 0, SEQS)
    return values.at[chosen].set(CACHE).astype(jnp.int32)


def place_ends(result, key, least, largest):
    dims = result.shape
    spot = [jax.random.randint(jax.random.fold_in(key, axis), (), 0, dims[axis]) for axis in range(len(dims))]
    result = result.at[tuple(spot)].set(least)
    longest = dims.index(max(dims))
    spot[longest] = (spot[longest] + 1) % dims[longest]
    return result.at[tuple(spot)].set(largest)


def steps_of(key, shape, cuts, smallest, top_value):
    factor_of = 1.0
    for dim, parts in cuts:
        draws = jax.random.uniform(jax.random.fold_in(jax.random.fold_in(key, 6), dim), (parts,), jnp.float32, smallest / len(cuts), top_value / len(cuts))
        factor_of = factor_of * jnp.repeat(jnp.exp(draws), shape[dim] // parts).reshape((-1,) + (1,) * (len(shape) - 1 - dim))
    return factor_of


def gaussian(rng, dims, scale, reach, shards=(), dtype=jnp.bfloat16):
    values = scale * jax.random.normal(rng, dims, jnp.float32)
    if shards:
        values = values * steps_of(rng, dims, shards, -0.22, 0.18)
    return jnp.clip(values, -reach, reach).astype(dtype)


def setup_inputs(seed: int = 0) -> dict:
    seeds = jax.random.split(jax.random.key(seed), 13)
    tokens = draw_tokens(jax.random.fold_in(seeds[12], 71), 0)
    ln_gain = jnp.clip(1.0 + 0.18 * jax.random.normal(seeds[1], (D,), jnp.float32), 0.099609375, 1.8984375).astype(jnp.bfloat16)
    w_gate = gaussian(seeds[2], (D, FF), D ** -0.5, 0.046875, ((0, 16), (1, 16)))
    w_up = gaussian(seeds[3], (D, FF), D ** -0.5, 0.046875, ((0, 16), (1, 16)))
    w_down = gaussian(seeds[4], (FF, D), FF ** -0.5, 0.0546875, ((0, 16), (1, 16)))
    w_query = gaussian(seeds[5], (D, HEADS * HEAD_DIM), (D // 16) ** -0.5, 0.1875, ((0, 16), (1, 16)))
    w_kv = gaussian(seeds[6], (D, 2 * HEAD_DIM), D ** -0.5, 0.046875, ((0, 16),))
    w_out = gaussian(seeds[7], (HEADS * HEAD_DIM, D), (HEADS * HEAD_DIM) ** -0.5, 0.0546875, ((0, 16), (1, 16)))
    cache_keys = draw_cache_keys(jax.random.fold_in(seeds[12], 71), 0)
    cache_values = gaussian(seeds[9], (SEQS, CACHE, HEAD_DIM), 1.0, 6.0, ((0, 256),))
    lengths = draw_lengths(jax.random.fold_in(seeds[12], 71), 0)
    positions = place_ends(jax.random.randint(seeds[11], (SEQS,), 0, 8192), jax.random.fold_in(seeds[11], 1), 0, 8191).astype(jnp.int32)
    return {"tokens": tokens, "ln_gain": ln_gain, "w_gate": w_gate, "w_up": w_up, "w_down": w_down, "w_query": w_query, "w_kv": w_kv, "w_out": w_out, "cache_keys": cache_keys, "cache_values": cache_values, "lengths": lengths, "positions": positions}


def layer_norm(tokens, ln_gain):
    values = tokens.astype(jnp.float32)
    center = lax.optimization_barrier(jnp.mean(values, axis=-1, keepdims=True))
    spread = lax.optimization_barrier(jnp.mean(values * values, axis=-1, keepdims=True)) - center * center
    return ((values - center) * lax.rsqrt(spread + 1e-05) * ln_gain.astype(jnp.float32)).astype(jnp.bfloat16)

def rotate(vector, place):
    half = vector.shape[-1] // 2
    freq = 10000.0 ** (-(jnp.arange(half).astype(jnp.float32) * 2.0 / vector.shape[-1]))
    angle = place[..., None].astype(jnp.float32) * freq
    first = vector[..., :half]
    second = vector[..., half:]
    return jnp.concatenate([first * jnp.cos(angle) - second * jnp.sin(angle), first * jnp.sin(angle) + second * jnp.cos(angle)], axis=-1)

def attend(query, fresh, keys_old, values_old, length, start):
    width = keys_old.shape[-1]
    count = query.shape[0]
    step_ids = jnp.arange(count).astype(jnp.int32)
    place = start + step_ids
    qrot = rotate(query.astype(jnp.float32), place[:, None])
    krot = rotate(fresh[:, :width].astype(jnp.float32), place)
    keys = jnp.concatenate([keys_old.astype(jnp.float32), krot], axis=0)
    values = jnp.concatenate([values_old, fresh[:, width:]], axis=0)
    scores = jnp.einsum('thd,kd->thk', qrot, keys, precision=lax.Precision.HIGHEST) / jnp.sqrt(jnp.float32(width))
    column = jnp.arange(keys.shape[0]).astype(jnp.int32)
    slots = keys_old.shape[0]
    visible = jnp.where(column[None, :] < slots, column[None, :] < length, column[None, :] - slots <= step_ids[:, None])
    scores = jnp.where(visible[:, None, :], scores, -jnp.inf)
    top = lax.optimization_barrier(jnp.max(scores, axis=-1, keepdims=True))
    weights = jnp.exp(scores - top)
    probs = (weights / lax.optimization_barrier(jnp.sum(weights, axis=-1, keepdims=True))).astype(jnp.bfloat16)
    return jnp.einsum('thk,kd->thd', probs.astype(jnp.float32), values.astype(jnp.float32)).astype(jnp.bfloat16)

def reference(tokens, ln_gain, w_gate, w_up, w_down, w_query, w_kv, w_out, cache_keys, cache_values, lengths, positions):
    rows = SEQS * DRAFT
    normed = layer_norm(tokens, ln_gain).reshape(rows, D)
    gate = jnp.dot(normed, w_gate, preferred_element_type=jnp.float32)
    up_part = jnp.dot(normed, w_up, preferred_element_type=jnp.float32)
    hidden = (jax.nn.silu(gate) * up_part).astype(jnp.bfloat16)
    query = jnp.dot(normed, w_query, preferred_element_type=jnp.float32).astype(jnp.bfloat16).reshape(SEQS, DRAFT, HEADS, HEAD_DIM)
    fresh = jnp.dot(normed, w_kv, preferred_element_type=jnp.float32).astype(jnp.bfloat16).reshape(SEQS, DRAFT, 2 * HEAD_DIM)

    def one_sequence(items):
        return attend(*items)
    context = lax.map(one_sequence, (query, fresh, cache_keys, cache_values, lengths, positions))
    mixed = jnp.dot(context.reshape(rows, HEADS * HEAD_DIM), w_out, preferred_element_type=jnp.float32)
    mixed = mixed + jnp.dot(hidden, w_down, preferred_element_type=jnp.float32)
    return (tokens.astype(jnp.float32) + mixed.reshape(SEQS, DRAFT, D)).astype(jnp.bfloat16)
```

```python
import jax
import jax.numpy as jnp
from jax import lax
from jax.experimental import pallas as pl
from jax.experimental.pallas import tpu as pltpu
from jax.sharding import Mesh, PartitionSpec as P

F32 = jnp.float32
BF16 = jnp.bfloat16
SIZES = {"zl": 4, "x": 4, "zh": 2, "y": 4, "c": 2}


def swap(a, axis, mask):
    return lax.ppermute(a, axis, [(i, i ^ mask) for i in range(SIZES[axis])])


def row_order(me):
    row = lax.broadcasted_iota(jnp.int32, (256, 256), 0)
    col = lax.broadcasted_iota(jnp.int32, (256, 256), 1)
    code = (row >> 5) & 3
    k = ((row >> 4) & 1) * 8 + (code ^ (code >> 1)) * 2 + (row >> 7)
    same = ((row >> 2) & 3) == (col >> 6)
    same = same & ((row & 3) == (col & 3))
    return (same & (((col >> 2) & 15) == (k ^ me))).astype(BF16)


def pair_order():
    row = lax.broadcasted_iota(jnp.int32, (64, 64), 0)
    col = lax.broadcasted_iota(jnp.int32, (64, 64), 1)
    same = ((row >> 4) == ((col >> 2) & 3)) & (((row >> 2) & 3) == (col >> 4))
    return (same & ((row & 3) == (col & 3))).astype(BF16)


def pick(order, rows):
    return jnp.dot(order, rows, preferred_element_type=F32).astype(BF16)


def attend_kernel(length, query, cos, sin, krot, vnew, keys, values, out):
    heads = query.shape[1] // 256
    rows = query.shape[0]
    c = cos[...]
    s = sin[...]
    parts = []
    for h in range(heads):
        q = query[:, h * 256 : (h + 1) * 256].astype(F32)
        a = q[:, :128]
        b = q[:, 128:]
        parts.append(jnp.concatenate([a * c - b * s, a * s + b * c], axis=1))
    q = jnp.concatenate(parts, axis=0) * (1.0 / 16.0)
    n = heads * rows
    q0 = q.astype(BF16)
    rest = q - q0.astype(F32)
    q1 = rest.astype(BF16)
    q2 = (rest - q1.astype(F32)).astype(BF16)
    dims = (((1,), (1,)), ((), ()))
    k = keys[0]
    old = (
        lax.dot_general(q2, k, dims, preferred_element_type=F32)
        + lax.dot_general(q1, k, dims, preferred_element_type=F32)
    ) + lax.dot_general(q0, k, dims, preferred_element_type=F32)
    new = lax.dot_general(
        q, krot[...], dims, precision=lax.Precision.HIGHEST, preferred_element_type=F32
    )
    slot = lax.broadcasted_iota(jnp.int32, old.shape, 1)
    old = jnp.where(slot < length[0], old, -jnp.inf)
    step = lax.broadcasted_iota(jnp.int32, new.shape, 0) & 3
    place = lax.broadcasted_iota(jnp.int32, new.shape, 1)
    new = jnp.where(place <= step, new, -jnp.inf)
    top = jnp.maximum(jnp.max(old, axis=1, keepdims=True), jnp.max(new, axis=1, keepdims=True))
    old = jnp.exp(old - top)
    new = jnp.exp(new - top)
    total = jnp.sum(old, axis=1, keepdims=True) + jnp.sum(new, axis=1, keepdims=True)
    old = (old / total).astype(BF16)
    new = (new / total).astype(BF16)
    mixed = jnp.dot(old, values[0], preferred_element_type=F32) + jnp.dot(
        new, vnew[...], preferred_element_type=F32
    )
    mixed = mixed.astype(BF16)
    for h in range(heads):
        out[:, h * 256 : (h + 1) * 256] = mixed[h * rows : (h + 1) * rows]


def attend(query, cos, sin, krot, vnew, keys, values, length):
    spec = pl.BlockSpec(memory_space=pltpu.VMEM)
    return pl.pallas_call(
        attend_kernel,
        out_shape=jax.ShapeDtypeStruct(query.shape, BF16),
        in_specs=[pl.BlockSpec(memory_space=pltpu.SMEM)] + [spec] * 7,
        out_specs=spec,
        compiler_params=pltpu.CompilerParams(vmem_limit_bytes=32 * 1024 * 1024),
        cost_estimate=pl.CostEstimate(
            flops=2_000_000_000, bytes_accessed=2_400_000, transcendentals=400_000
        ),
        name="attend",
    )(length, query, cos, sin, krot, vnew, keys, values)


def scatter_y(a, first):
    if first == 1:
        a = a.reshape(a.shape[0], 2, 2, *a.shape[2:])
        got = swap(a[:, :, 1].astype(BF16), "y", 1)
        a = a[:, :, 0] + got.astype(F32)
    else:
        got = swap(a[:, 2:].astype(BF16), "y", 3)
        a = a[:, :2] + got.astype(F32)
    got = swap(a[:, 1].astype(BF16), "y", 4 - first)
    a = a[:, 0] + got.astype(F32)
    got = swap(a[:, 1].astype(BF16), "zh", 1)
    return a[:, 0] + got.astype(F32)


def gather_emb(a):
    b = swap(a, "zh", 1)
    a1 = swap(a, "y", 1)
    a3 = swap(a, "y", 3)
    b3 = swap(b, "y", 3)
    b1 = swap(b, "y", 1)
    a2 = swap(a1, "y", 3)
    b2 = swap(b3, "y", 1)
    mine = jnp.stack([a, b, a1, b1, a3, b3, a2, b2])
    mine = mine.reshape(4, 2, *a.shape)
    return mine, swap(mine, "c", 1)


def body(
    tokens,
    ln_gain,
    w_gate,
    w_up,
    w_down,
    w_query,
    w_kv,
    w_out,
    cache_keys,
    cache_values,
    lengths,
    positions,
):
    width = tokens.shape[2]
    total = width * 16
    me = lax.axis_index("zh") * 8 + lax.axis_index("y") * 2 + lax.axis_index("c")
    own = tokens.reshape(64, width)
    order = row_order(me)
    turn = pair_order()

    vals = own.astype(F32)
    stat = jnp.stack([jnp.sum(vals, axis=1), jnp.sum(vals * vals, axis=1)])
    tz = [own] + [swap(own, "zl", m) for m in (1, 2, 3)]
    stat = stat + swap(stat, "c", 1)
    stat = stat + swap(stat, "y", 1)
    stat = stat + swap(stat, "y", 3)
    stat = stat + swap(stat, "zh", 1)
    sz = [stat] + [swap(stat, "zl", m) for m in (1, 2, 3)]
    gain = ln_gain.astype(F32)[None, :]
    rows = []
    for t, s in zip(tz, sz):
        center = s[0] / total
        spread = s[1] / total - center * center
        scale = lax.rsqrt(spread + 1e-05)
        rows.append(((t.astype(F32) - center[:, None]) * scale[:, None] * gain).astype(BF16))
    n0 = pick(order, jnp.concatenate(rows, axis=0))

    a, b = n0[:128], n0[128:]
    a1 = swap(a, "x", 1)
    b3 = swap(b, "x", 3)
    a3 = swap(a, "x", 3)
    b1 = swap(b, "x", 1)
    a2 = swap(a1, "x", 3)
    b2 = swap(b3, "x", 1)
    rows_a = jnp.concatenate([a, a1, a2, a3], axis=0)
    rows_b = jnp.concatenate([b, b1, b2, b3], axis=0)

    kv = jnp.dot(n0, w_kv, preferred_element_type=F32).reshape(2, 1, 4, 2, 16, 512)
    kv = kv[0] + swap(kv[1].astype(BF16), "c", 1).astype(F32)
    fresh = scatter_y(kv, 1)[0, :4].astype(BF16)
    angle = (positions + jnp.arange(4)).astype(F32)[:, None] * (
        10000.0 ** (-(jnp.arange(128).astype(F32) * 2.0 / 256))
    )
    cos, sin = jnp.cos(angle), jnp.sin(angle)
    ka, kc = fresh[:, :128].astype(F32), fresh[:, 128:256].astype(F32)
    krot = jnp.concatenate([ka * cos - kc * sin, ka * sin + kc * cos], axis=1)
    krot = jnp.pad(krot, ((0, 124), (0, 0)))
    vnew = jnp.pad(fresh[:, 256:], ((0, 124), (0, 0)))
    cos64, sin64 = jnp.tile(cos, (16, 1)), jnp.tile(sin, (16, 1))

    def project(w):
        away = jnp.dot(rows_b, w, preferred_element_type=F32).astype(BF16)
        got = swap(away, "c", 1)
        kept = jnp.dot(rows_a, w, preferred_element_type=F32)
        return (kept + got.astype(F32)).reshape(4, 4, 2, 16, w.shape[1])

    q = project(w_query)
    half = q.shape[-1] // 2
    query = jnp.concatenate(
        [scatter_y(q[..., :half], 1), scatter_y(q[..., half:], 3)], axis=-1
    ).astype(BF16)
    gate = scatter_y(project(w_gate), 1)
    up = scatter_y(project(w_up), 3)
    hidden = (jax.nn.silu(gate) * up).astype(BF16).reshape(64, -1)

    q = jnp.concatenate([query[0]] + [swap(query[m], "x", m) for m in (1, 2, 3)], axis=0)
    q = pick(turn, q).reshape(4, 16, -1)
    q = jnp.concatenate([q[0]] + [swap(q[m], "zl", m) for m in (1, 2, 3)], axis=0)
    ctx = attend(q, cos64, sin64, krot, vnew, cache_keys, cache_values, lengths)
    ctx = ctx.reshape(4, 16, -1)
    ctx = jnp.concatenate([ctx[0]] + [swap(ctx[m], "zl", m) for m in (1, 2, 3)], axis=0)
    ctx = pick(turn, ctx).reshape(4, 16, -1)
    ctx = jnp.concatenate([ctx[0]] + [swap(ctx[m], "x", m) for m in (1, 2, 3)], axis=0)

    hid_a, hid_b = gather_emb(hidden)
    ctx_a, ctx_b = gather_emb(ctx)

    def product(c, h):
        c = c.reshape(512, -1)
        h = h.reshape(512, -1)
        r = jnp.dot(h, w_down, preferred_element_type=F32)
        r = r + jnp.dot(c, w_out, preferred_element_type=F32)
        return r.reshape(8, 4, 16, width)

    ra = product(ctx_a, hid_a)
    rb = product(ctx_b, hid_b)
    got = swap(ra[:, 1:3].astype(BF16), "x", 1)
    ga = swap(rb[:, 2:].astype(BF16), "x", 3)
    a0, a3 = ra[:, 0] + got[:, 0].astype(F32), ra[:, 3] + got[:, 1].astype(F32)
    b0, b1 = rb[:, 0] + ga[:, 1].astype(F32), rb[:, 1] + ga[:, 0].astype(F32)
    a0 = a0 + swap(a3.astype(BF16), "x", 3).astype(F32)
    b0 = b0 + swap(b1.astype(BF16), "x", 1).astype(F32)
    r = jnp.concatenate([a0.reshape(128, width), b0.reshape(128, width)], axis=0).astype(BF16)
    r = lax.dot_general(order, r, (((0,), (0,)), ((), ())), preferred_element_type=F32)
    r = r.astype(BF16).reshape(4, 64, width)
    mixed = r[0].astype(F32)
    for m in (1, 2, 3):
        mixed = mixed + swap(r[m], "zl", m).astype(F32)
    return (vals + mixed).astype(BF16).reshape(tokens.shape)


def solution(mesh):
    fine = Mesh(mesh.devices.reshape(4, 4, 2, 4, 2), ("zl", "x", "zh", "y", "c"))
    ffn = ("zl", "x")
    emb = ("zh", "y", "c")
    every = ffn + emb
    placed = (
        P(ffn, None, emb),
        P(emb),
        P(emb, ffn),
        P(emb, ffn),
        P(ffn, emb),
        P(emb, ffn),
        P(emb, None),
        P(ffn, emb),
        P(every, None, None),
        P(every, None, None),
        P(every),
        P(every),
    )
    return jax.shard_map(
        body, mesh=fine, in_specs=placed, out_specs=P(ffn, None, emb), check_vma=False
    )
```

```python
import jax
import jax.numpy as jnp
from jax import lax
from jax.experimental import pallas as pl
from jax.experimental.pallas import tpu as pltpu
from jax.sharding import Mesh, PartitionSpec as P

F32 = jnp.float32
BF16 = jnp.bfloat16
SIZES = {"zl": 4, "x": 4, "zh": 2, "y": 4, "c": 2}


def swap(a, axis, mask):
    return lax.ppermute(a, axis, [(i, i ^ mask) for i in range(SIZES[axis])])


def row_order(me):
    row = lax.broadcasted_iota(jnp.int32, (256, 256), 0)
    col = lax.broadcasted_iota(jnp.int32, (256, 256), 1)
    code = (row >> 5) & 3
    k = ((row >> 4) & 1) * 8 + (code ^ (code >> 1)) * 2 + (row >> 7)
    same = ((row >> 2) & 3) == (col >> 6)
    same = same & ((row & 3) == (col & 3))
    return (same & (((col >> 2) & 15) == (k ^ me))).astype(BF16)


def pair_order():
    row = lax.broadcasted_iota(jnp.int32, (64, 64), 0)
    col = lax.broadcasted_iota(jnp.int32, (64, 64), 1)
    same = ((row >> 4) == ((col >> 2) & 3)) & (((row >> 2) & 3) == (col >> 4))
    return (same & ((row & 3) == (col & 3))).astype(BF16)


def pick(order, rows):
    return jnp.dot(order, rows, preferred_element_type=F32).astype(BF16)


def attend_kernel(length, query, cos, sin, krot, vnew, keys, values, out):
    heads = query.shape[1] // 256
    rows = query.shape[0]
    c = cos[...]
    s = sin[...]
    parts = []
    for h in range(heads):
        q = query[:, h * 256 : (h + 1) * 256].astype(F32)
        a = q[:, :128]
        b = q[:, 128:]
        parts.append(jnp.concatenate([a * c - b * s, a * s + b * c], axis=1))
    q = jnp.concatenate(parts, axis=0) * (1.0 / 16.0)
    n = heads * rows
    q0 = q.astype(BF16)
    rest = q - q0.astype(F32)
    q1 = rest.astype(BF16)
    q2 = (rest - q1.astype(F32)).astype(BF16)
    dims = (((1,), (1,)), ((), ()))
    k = keys[0]
    old = (
        lax.dot_general(q2, k, dims, preferred_element_type=F32)
        + lax.dot_general(q1, k, dims, preferred_element_type=F32)
    ) + lax.dot_general(q0, k, dims, preferred_element_type=F32)
    new = lax.dot_general(
        q, krot[...], dims, precision=lax.Precision.HIGHEST, preferred_element_type=F32
    )
    slot = lax.broadcasted_iota(jnp.int32, old.shape, 1)
    old = jnp.where(slot < length[0], old, -jnp.inf)
    step = lax.broadcasted_iota(jnp.int32, new.shape, 0) & 3
    place = lax.broadcasted_iota(jnp.int32, new.shape, 1)
    new = jnp.where(place <= step, new, -jnp.inf)
    top = jnp.maximum(jnp.max(old, axis=1, keepdims=True), jnp.max(new, axis=1, keepdims=True))
    old = jnp.exp(old - top)
    new = jnp.exp(new - top)
    total = jnp.sum(old, axis=1, keepdims=True) + jnp.sum(new, axis=1, keepdims=True)
    old = (old / total).astype(BF16)
    new = (new / total).astype(BF16)
    mixed = jnp.dot(old, values[0], preferred_element_type=F32) + jnp.dot(
        new, vnew[...], preferred_element_type=F32
    )
    mixed = mixed.astype(BF16)
    for h in range(heads):
        out[:, h * 256 : (h + 1) * 256] = mixed[h * rows : (h + 1) * rows]


def attend(query, cos, sin, krot, vnew, keys, values, length):
    spec = pl.BlockSpec(memory_space=pltpu.VMEM)
    return pl.pallas_call(
        attend_kernel,
        out_shape=jax.ShapeDtypeStruct(query.shape, BF16),
        in_specs=[pl.BlockSpec(memory_space=pltpu.SMEM)] + [spec] * 7,
        out_specs=spec,
        compiler_params=pltpu.CompilerParams(vmem_limit_bytes=32 * 1024 * 1024),
        cost_estimate=pl.CostEstimate(
            flops=2_000_000_000, bytes_accessed=2_400_000, transcendentals=400_000
        ),
        name="attend",
    )(length, query, cos, sin, krot, vnew, keys, values)


def tie(a, b):
    return lax.optimization_barrier((a, b))


def step_y(a, first):
    if first == 1:
        a = a.reshape(a.shape[0], 2, 2, *a.shape[2:])
        return a[:, :, 0], swap(a[:, :, 1].astype(BF16), "y", 1)
    return a[:, :2], swap(a[:, 2:].astype(BF16), "y", 3)


def scatter_y(a, first):
    a, got = step_y(a, first)
    a = a + got.astype(F32)
    got = swap(a[:, 1].astype(BF16), "y", 4 - first)
    return a[:, 0] + got.astype(F32)


def scatter_zh(a):
    got = swap(a[:, 1].astype(BF16), "zh", 1)
    return a[:, 0] + got.astype(F32)


def exchange_x(blocks):
    got = swap(jnp.stack([blocks[1], blocks[3]]), "x", 1)
    far = swap(jnp.stack([blocks[2], got[1]]), "x", 3)
    return jnp.concatenate([blocks[0], got[0], far[0], far[1]], axis=0)


def exchange_z(blocks):
    got = swap(jnp.stack([blocks[1], blocks[3]]), "zl", 1)
    far = swap(jnp.stack([blocks[2], got[1]]), "zl", 2)
    return jnp.concatenate([blocks[0], got[0], far[0], far[1]], axis=0)


def both(a, axis, mask):
    return jnp.concatenate([a, swap(a, axis, mask)], axis=0)


def body(
    tokens,
    ln_gain,
    w_gate,
    w_up,
    w_down,
    w_query,
    w_kv,
    w_out,
    cache_keys,
    cache_values,
    lengths,
    positions,
):
    width = tokens.shape[2]
    total = width * 16
    me = lax.axis_index("zh") * 8 + lax.axis_index("y") * 2 + lax.axis_index("c")
    own = tokens.reshape(64, width)
    order = row_order(me)
    turn = pair_order()
    gain = ln_gain.astype(F32)[None, :]

    near = jnp.concatenate([own] + [swap(own, "zl", m) for m in (1, 2, 3)], axis=0)
    vals = own.astype(F32)
    stat = jnp.stack([jnp.sum(vals, axis=1), jnp.sum(vals * vals, axis=1)])
    stat = stat + swap(stat, "c", 1)
    stat = stat + swap(stat, "y", 1)
    stat = stat + swap(stat, "y", 3)
    stat = stat + swap(stat, "zh", 1)

    stat = both(both(stat[None], "zl", 1), "zl", 2)
    stat = jnp.concatenate(list(stat), axis=1)
    center = stat[0] / total
    scale = lax.rsqrt(stat[1] / total - center * center + 1e-05)
    near = (near.astype(F32) - center[:, None]) * scale[:, None] * gain
    n0 = pick(order, near.astype(BF16))

    rows_a, rows_b = n0[:128], n0[128:]
    pair_a = both(rows_a, "x", 1)
    pair_b = both(rows_b, "x", 3)
    pair_a, pair_b = lax.optimization_barrier((pair_a, pair_b))
    rows_a = both(pair_a, "x", 3)
    rows_b = both(pair_b, "x", 1)
    rows_b = rows_b.reshape(4, 128, width)
    rows_b = jnp.stack([rows_b[0], rows_b[2], rows_b[1], rows_b[3]]).reshape(512, width)

    def away(*ws):
        parts = [jnp.dot(rows_b, w, preferred_element_type=F32).astype(BF16) for w in ws]
        return jnp.concatenate(parts, axis=1)

    def add(got, *ws):
        kept = [jnp.dot(rows_a, w, preferred_element_type=F32) for w in ws]
        part = jnp.concatenate(kept, axis=1) + got.astype(F32)
        return part.reshape(4, 4, 2, 16, part.shape[1])

    def fresh_part(rows):
        part = jnp.dot(rows, w_kv, preferred_element_type=F32)
        return jnp.concatenate([part[:, i * 128 : (i + 1) * 128] for i in range(4)], axis=0)

    q_away = jnp.concatenate([away(w_query), fresh_part(n0[128:]).astype(BF16)], axis=1)
    q_got = swap(q_away, "c", 1)
    gu_away = away(w_gate, w_up)
    q_got, gu_away = tie(q_got, gu_away)
    width_q = w_query.shape[1]
    q = add(q_got[:, :width_q], w_query)
    kv = fresh_part(n0[:128]) + q_got[:, width_q:].astype(F32)
    q = jnp.concatenate([q, kv.reshape(4, 4, 2, 16, 128)], axis=-1)
    gu = add(swap(gu_away, "c", 1), w_gate, w_up)
    half = width_q // 2
    ff = w_gate.shape[1]
    q_a, a_sent = step_y(q[..., :half], 1)
    q_b, b_sent = step_y(q[..., half:], 3)
    a_sent, gu = tie(a_sent, gu)
    q_a = q_a + a_sent.astype(F32)
    q_b = q_b + b_sent.astype(F32)
    q_a = q_a[:, 0] + swap(q_a[:, 1].astype(BF16), "y", 3).astype(F32)
    q_b = q_b[:, 0] + swap(q_b[:, 1].astype(BF16), "y", 1).astype(F32)
    query = scatter_zh(jnp.concatenate([q_a, q_b], axis=-1))
    fresh = jnp.concatenate([query[i, :4, width_q:] for i in range(4)], axis=1).astype(BF16)
    query = query[..., :width_q].astype(BF16)
    gu, gu_sent = step_y(gu, 1)

    angle = (positions + jnp.arange(4)).astype(F32)[:, None] * (
        10000.0 ** (-(jnp.arange(128).astype(F32) * 2.0 / 256))
    )
    cos, sin = jnp.cos(angle), jnp.sin(angle)
    ka, kc = fresh[:, :128].astype(F32), fresh[:, 128:256].astype(F32)
    krot = jnp.concatenate([ka * cos - kc * sin, ka * sin + kc * cos], axis=1)
    krot = jnp.pad(krot, ((0, 124), (0, 0)))
    vnew = jnp.pad(fresh[:, 256:], ((0, 124), (0, 0)))
    cos64, sin64 = jnp.tile(cos, (16, 1)), jnp.tile(sin, (16, 1))

    q = pick(turn, exchange_x(query)).reshape(4, 16, -1)
    q, gu_sent = tie(q, gu_sent)
    gu = gu + gu_sent.astype(F32)
    gu_sent = swap(gu[:, 1].astype(BF16), "y", 3)
    q = exchange_z(q)
    q, gu_sent = tie(q, gu_sent)
    ctx = attend(q, cos64, sin64, krot, vnew, cache_keys, cache_values, lengths)
    gu = gu[:, 0] + gu_sent.astype(F32)
    gu_sent = swap(gu[:, 1].astype(BF16), "zh", 1)
    gu = (gu[:, 0] + gu_sent.astype(F32)).reshape(64, -1)
    hidden = (jax.nn.silu(gu[:, :ff]) * gu[:, ff:]).astype(BF16)
    ctx = pick(turn, exchange_z(ctx.reshape(4, 16, -1))).reshape(4, 16, -1)
    ctx = exchange_x(ctx)

    mine = jnp.concatenate([ctx, hidden], axis=1)[None]
    other = swap(mine, "zh", 1)
    mine = both(both(mine, "y", 1), "y", 3)
    other = both(both(other, "y", 1), "y", 3)
    here = jnp.stack([mine, other], axis=1).reshape(512, -1)
    there = swap(here, "c", 1)

    def product(r):
        split = w_out.shape[0]
        o = jnp.dot(r[:, :split], w_out, preferred_element_type=F32)
        o = o + jnp.dot(r[:, split:], w_down, preferred_element_type=F32)
        return o.reshape(8, 4, 16, width)

    ra = product(here)
    there, ra = tie(there, ra)
    rb = product(there)
    ra = ra.reshape(8, 2, 2, 16, width)
    ra = ra[:, :, 0] + swap(ra[:, :, 1].astype(BF16), "x", 1).astype(F32)
    rb = rb[:, :2] + swap(rb[:, 2:].astype(BF16), "x", 3).astype(F32)
    ra = ra[:, 0] + swap(ra[:, 1].astype(BF16), "x", 3).astype(F32)
    rb = rb[:, 0] + swap(rb[:, 1].astype(BF16), "x", 1).astype(F32)
    r = jnp.concatenate([ra.reshape(128, width), rb.reshape(128, width)], axis=0).astype(BF16)
    r = lax.dot_general(order, r, (((0,), (0,)), ((), ())), preferred_element_type=F32)
    r = r.astype(BF16).reshape(4, 64, width)
    mixed = r[0].astype(F32)
    for m in (1, 2, 3):
        mixed = mixed + swap(r[m], "zl", m).astype(F32)
    return (vals + mixed).astype(BF16).reshape(tokens.shape)


def solution(mesh):
    fine = Mesh(mesh.devices.reshape(4, 4, 2, 4, 2), ("zl", "x", "zh", "y", "c"))
    ffn = ("zl", "x")
    emb = ("zh", "y", "c")
    every = ffn + emb
    placed = (
        P(ffn, None, emb),
        P(emb),
        P(emb, ffn),
        P(emb, ffn),
        P(ffn, emb),
        P(emb, ffn),
        P(emb, None),
        P(ffn, emb),
        P(every, None, None),
        P(every, None, None),
        P(every),
        P(every),
    )
    return jax.shard_map(
        body, mesh=fine, in_specs=placed, out_specs=P(ffn, None, emb), check_vma=False
    )
```

```python
import jax
import jax.numpy as jnp
from jax import lax
from jax.experimental import pallas as pl
from jax.experimental.pallas import tpu as pltpu
from jax.sharding import Mesh, PartitionSpec as P

F32 = jnp.float32
BF16 = jnp.bfloat16
SIZES = {"zl": 4, "x": 4, "zh": 2, "y": 4, "c": 2}


def swap(a, axis, mask):
    return lax.ppermute(a, axis, [(i, i ^ mask) for i in range(SIZES[axis])])


def row_order(me):
    row = lax.broadcasted_iota(jnp.int32, (256, 256), 0)
    col = lax.broadcasted_iota(jnp.int32, (256, 256), 1)
    code = (row >> 5) & 3
    k = ((row >> 4) & 1) * 8 + (code ^ (code >> 1)) * 2 + (row >> 7)
    same = ((row >> 2) & 3) == (col >> 6)
    same = same & ((row & 3) == (col & 3))
    return (same & (((col >> 2) & 15) == (k ^ me))).astype(BF16)


def pair_order():
    row = lax.broadcasted_iota(jnp.int32, (64, 64), 0)
    col = lax.broadcasted_iota(jnp.int32, (64, 64), 1)
    same = ((row >> 4) == ((col >> 2) & 3)) & (((row >> 2) & 3) == (col >> 4))
    return (same & ((row & 3) == (col & 3))).astype(BF16)


def pick(order, rows):
    return jnp.dot(order, rows, preferred_element_type=F32).astype(BF16)


def attend_kernel(length, query, cos, sin, krot, vnew, keys, values, out):
    heads = query.shape[1] // 256
    rows = query.shape[0]
    c = cos[...]
    s = sin[...]
    parts = []
    for h in range(heads):
        q = query[:, h * 256 : (h + 1) * 256].astype(F32)
        a = q[:, :128]
        b = q[:, 128:]
        parts.append(jnp.concatenate([a * c - b * s, a * s + b * c], axis=1))
    q = jnp.concatenate(parts, axis=0) * (1.0 / 16.0)
    n = heads * rows
    q0 = q.astype(BF16)
    rest = q - q0.astype(F32)
    q1 = rest.astype(BF16)
    q2 = (rest - q1.astype(F32)).astype(BF16)
    dims = (((1,), (1,)), ((), ()))
    k = keys[0]
    old = (
        lax.dot_general(q2, k, dims, preferred_element_type=F32)
        + lax.dot_general(q1, k, dims, preferred_element_type=F32)
    ) + lax.dot_general(q0, k, dims, preferred_element_type=F32)
    new = lax.dot_general(
        q, krot[...], dims, precision=lax.Precision.HIGHEST, preferred_element_type=F32
    )
    slot = lax.broadcasted_iota(jnp.int32, old.shape, 1)
    old = jnp.where(slot < length[0], old, -jnp.inf)
    step = lax.broadcasted_iota(jnp.int32, new.shape, 0) & 3
    place = lax.broadcasted_iota(jnp.int32, new.shape, 1)
    new = jnp.where(place <= step, new, -jnp.inf)
    top = jnp.maximum(jnp.max(old, axis=1, keepdims=True), jnp.max(new, axis=1, keepdims=True))
    old = jnp.exp(old - top)
    new = jnp.exp(new - top)
    total = jnp.sum(old, axis=1, keepdims=True) + jnp.sum(new, axis=1, keepdims=True)
    old = (old / total).astype(BF16)
    new = (new / total).astype(BF16)
    mixed = jnp.dot(old, values[0], preferred_element_type=F32) + jnp.dot(
        new, vnew[...], preferred_element_type=F32
    )
    mixed = mixed.astype(BF16)
    for h in range(heads):
        out[:, h * 256 : (h + 1) * 256] = mixed[h * rows : (h + 1) * rows]


def attend(query, cos, sin, krot, vnew, keys, values, length):
    spec = pl.BlockSpec(memory_space=pltpu.VMEM)
    return pl.pallas_call(
        attend_kernel,
        out_shape=jax.ShapeDtypeStruct(query.shape, BF16),
        in_specs=[pl.BlockSpec(memory_space=pltpu.SMEM)] + [spec] * 7,
        out_specs=spec,
        compiler_params=pltpu.CompilerParams(vmem_limit_bytes=32 * 1024 * 1024),
        cost_estimate=pl.CostEstimate(
            flops=2_000_000_000, bytes_accessed=2_400_000, transcendentals=400_000
        ),
        name="attend",
    )(length, query, cos, sin, krot, vnew, keys, values)


def tie(a, b):
    return lax.optimization_barrier((a, b))


def step_y(a, first):
    if first == 1:
        a = a.reshape(a.shape[0], 2, 2, *a.shape[2:])
        return a[:, :, 0], swap(a[:, :, 1].astype(BF16), "y", 1)
    return a[:, :2], swap(a[:, 2:].astype(BF16), "y", 3)


def scatter_y(a, first):
    a, got = step_y(a, first)
    a = a + got.astype(F32)
    got = swap(a[:, 1].astype(BF16), "y", 4 - first)
    return a[:, 0] + got.astype(F32)


def scatter_zh(a):
    got = swap(a[:, 1].astype(BF16), "zh", 1)
    return a[:, 0] + got.astype(F32)


def exchange_x(blocks):
    got = swap(jnp.stack([blocks[1], blocks[3]]), "x", 1)
    far = swap(jnp.stack([blocks[2], got[1]]), "x", 3)
    return jnp.concatenate([blocks[0], got[0], far[0], far[1]], axis=0)


def exchange_z(blocks):
    got = swap(jnp.stack([blocks[1], blocks[3]]), "zl", 1)
    far = swap(jnp.stack([blocks[2], got[1]]), "zl", 2)
    return jnp.concatenate([blocks[0], got[0], far[0], far[1]], axis=0)


def both(a, axis, mask):
    return jnp.concatenate([a, swap(a, axis, mask)], axis=0)


def body(
    tokens,
    ln_gain,
    w_gate,
    w_up,
    w_down,
    w_query,
    w_kv,
    w_out,
    cache_keys,
    cache_values,
    lengths,
    positions,
):
    width = tokens.shape[2]
    total = width * 16
    me = lax.axis_index("zh") * 8 + lax.axis_index("y") * 2 + lax.axis_index("c")
    own = tokens.reshape(64, width)
    order = row_order(me)
    turn = pair_order()
    gain = ln_gain.astype(F32)[None, :]

    near = jnp.concatenate([own] + [swap(own, "zl", m) for m in (1, 2, 3)], axis=0)
    vals = own.astype(F32)
    stat = jnp.stack([jnp.sum(vals, axis=1), jnp.sum(vals * vals, axis=1)])
    stat = stat + swap(stat, "c", 1)
    stat = stat + swap(stat, "y", 1)
    stat = stat + swap(stat, "y", 3)
    stat = stat + swap(stat, "zh", 1)

    n0 = pick(order, near)
    rows_a, rows_b = n0[:128], n0[128:]
    pair_a = both(rows_a, "x", 1)
    pair_b = both(rows_b, "x", 3)
    (pair_a, pair_b), stat = tie((pair_a, pair_b), stat)

    stat = both(both(stat[None], "zl", 1), "zl", 2)
    stat = jnp.concatenate(list(stat), axis=1)
    center = stat[0] / total
    stat = jnp.stack([center, lax.rsqrt(stat[1] / total - center * center + 1e-05)])
    stat = lax.dot_general(
        stat,
        order.astype(F32),
        (((1,), (1,)), ((), ())),
        precision=lax.Precision.HIGHEST,
        preferred_element_type=F32,
    )
    stats = both(both(stat[None], "x", 1), "x", 3)

    rows_a = both(pair_a, "x", 3)
    rows_b = both(pair_b, "x", 1)
    rows_b = rows_b.reshape(4, 128, width)
    rows_b = jnp.stack([rows_b[0], rows_b[2], rows_b[1], rows_b[3]]).reshape(512, width)

    def norm(rows, s):
        mid = jnp.concatenate([s[i, 0] for i in range(4)])[:, None]
        mul = jnp.concatenate([s[i, 1] for i in range(4)])[:, None]
        return ((rows.astype(F32) - mid) * mul * gain).astype(BF16)

    rows_a = norm(rows_a, stats[:, :, :128])
    rows_b = norm(rows_b, stats[:, :, 128:])
    rows_a, rows_b = tie(rows_a, rows_b)

    def away(*ws):
        parts = [jnp.dot(rows_b, w, preferred_element_type=F32).astype(BF16) for w in ws]
        return jnp.concatenate(parts, axis=1)

    def add(got, *ws):
        kept = [jnp.dot(rows_a, w, preferred_element_type=F32) for w in ws]
        part = jnp.concatenate(kept, axis=1) + got.astype(F32)
        return part.reshape(4, 4, 2, 16, part.shape[1])

    def fresh_part(rows):
        part = jnp.dot(rows, w_kv, preferred_element_type=F32)
        return jnp.concatenate([part[:, i * 128 : (i + 1) * 128] for i in range(4)], axis=0)

    q_away = jnp.concatenate([away(w_query), fresh_part(rows_b[:128]).astype(BF16)], axis=1)
    q_got = swap(q_away, "c", 1)
    gu_away = away(w_gate, w_up)
    q_got, gu_away = tie(q_got, gu_away)
    width_q = w_query.shape[1]
    q = add(q_got[:, :width_q], w_query)
    kv = fresh_part(rows_a[:128]) + q_got[:, width_q:].astype(F32)
    q = jnp.concatenate([q, kv.reshape(4, 4, 2, 16, 128)], axis=-1)
    gu = add(swap(gu_away, "c", 1), w_gate, w_up)
    half = width_q // 2
    ff = w_gate.shape[1]
    q_a, a_sent = step_y(q[..., :half], 1)
    q_b, b_sent = step_y(q[..., half:], 3)
    a_sent, gu = tie(a_sent, gu)
    q_a = q_a + a_sent.astype(F32)
    q_b = q_b + b_sent.astype(F32)
    q_a = q_a[:, 0] + swap(q_a[:, 1].astype(BF16), "y", 3).astype(F32)
    q_b = q_b[:, 0] + swap(q_b[:, 1].astype(BF16), "y", 1).astype(F32)
    query = scatter_zh(jnp.concatenate([q_a, q_b], axis=-1))
    fresh = jnp.concatenate([query[i, :4, width_q:] for i in range(4)], axis=1).astype(BF16)
    query = query[..., :width_q].astype(BF16)
    gu, gu_sent = step_y(gu, 1)

    angle = (positions + jnp.arange(4)).astype(F32)[:, None] * (
        10000.0 ** (-(jnp.arange(128).astype(F32) * 2.0 / 256))
    )
    cos, sin = jnp.cos(angle), jnp.sin(angle)
    ka, kc = fresh[:, :128].astype(F32), fresh[:, 128:256].astype(F32)
    krot = jnp.concatenate([ka * cos - kc * sin, ka * sin + kc * cos], axis=1)
    krot = jnp.pad(krot, ((0, 124), (0, 0)))
    vnew = jnp.pad(fresh[:, 256:], ((0, 124), (0, 0)))
    cos64, sin64 = jnp.tile(cos, (16, 1)), jnp.tile(sin, (16, 1))

    q = pick(turn, exchange_x(query)).reshape(4, 16, -1)
    q, gu_sent = tie(q, gu_sent)
    gu = gu + gu_sent.astype(F32)
    gu_sent = swap(gu[:, 1].astype(BF16), "y", 3)
    q = exchange_z(q)
    q, gu_sent = tie(q, gu_sent)
    ctx = attend(q, cos64, sin64, krot, vnew, cache_keys, cache_values, lengths)
    gu = gu[:, 0] + gu_sent.astype(F32)
    gu_sent = swap(gu[:, 1].astype(BF16), "zh", 1)
    gu = (gu[:, 0] + gu_sent.astype(F32)).reshape(64, -1)
    hidden = (jax.nn.silu(gu[:, :ff]) * gu[:, ff:]).astype(BF16)
    ctx = pick(turn, exchange_z(ctx.reshape(4, 16, -1))).reshape(4, 16, -1)
    ctx = exchange_x(ctx)

    mine = jnp.concatenate([ctx, hidden], axis=1)[None]
    other = swap(mine, "zh", 1)
    mine = both(both(mine, "y", 1), "y", 3)
    other = both(both(other, "y", 1), "y", 3)
    here = jnp.stack([mine, other], axis=1).reshape(512, -1)
    there = swap(here, "c", 1)

    def product(r):
        split = w_out.shape[0]
        o = jnp.dot(r[:, :split], w_out, preferred_element_type=F32)
        o = o + jnp.dot(r[:, split:], w_down, preferred_element_type=F32)
        return o.reshape(8, 4, 16, width)

    ra = product(here)
    there, ra = tie(there, ra)
    rb = product(there)
    ra = ra.reshape(8, 2, 2, 16, width)
    ra = ra[:, :, 0] + swap(ra[:, :, 1].astype(BF16), "x", 1).astype(F32)
    rb = rb[:, :2] + swap(rb[:, 2:].astype(BF16), "x", 3).astype(F32)
    ra = ra[:, 0] + swap(ra[:, 1].astype(BF16), "x", 3).astype(F32)
    rb = rb[:, 0] + swap(rb[:, 1].astype(BF16), "x", 1).astype(F32)
    r = jnp.concatenate([ra.reshape(128, width), rb.reshape(128, width)], axis=0).astype(BF16)
    r = lax.dot_general(order, r, (((0,), (0,)), ((), ())), preferred_element_type=F32)
    r = r.astype(BF16).reshape(4, 64, width)
    mixed = r[0].astype(F32)
    for m in (1, 2, 3):
        mixed = mixed + swap(r[m], "zl", m).astype(F32)
    return (vals + mixed).astype(BF16).reshape(tokens.shape)


def solution(mesh):
    fine = Mesh(mesh.devices.reshape(4, 4, 2, 4, 2), ("zl", "x", "zh", "y", "c"))
    ffn = ("zl", "x")
    emb = ("zh", "y", "c")
    every = ffn + emb
    placed = (
        P(ffn, None, emb),
        P(emb),
        P(emb, ffn),
        P(emb, ffn),
        P(ffn, emb),
        P(emb, ffn),
        P(emb, None),
        P(ffn, emb),
        P(every, None, None),
        P(every, None, None),
        P(every),
        P(every),
    )
    return jax.shard_map(
        body, mesh=fine, in_specs=placed, out_specs=P(ffn, None, emb), check_vma=False
    )
```

```python
import jax
import jax.numpy as jnp
from jax import lax
from jax.experimental import pallas as pl
from jax.experimental.pallas import tpu as pltpu
from jax.sharding import Mesh, PartitionSpec as P

F32 = jnp.float32
BF16 = jnp.bfloat16
SIZES = {"zl": 4, "x": 4, "zh": 2, "y": 4, "c": 2}


def swap(a, axis, mask):
    return lax.ppermute(a, axis, [(i, i ^ mask) for i in range(SIZES[axis])])


def row_order(me):
    row = lax.broadcasted_iota(jnp.int32, (256, 256), 0)
    col = lax.broadcasted_iota(jnp.int32, (256, 256), 1)
    code = (row >> 5) & 3
    k = ((row >> 4) & 1) * 8 + (code ^ (code >> 1)) * 2 + (row >> 7)
    same = ((row >> 2) & 3) == (col >> 6)
    same = same & ((row & 3) == (col & 3))
    return (same & (((col >> 2) & 15) == (k ^ me))).astype(BF16)


def pair_order():
    row = lax.broadcasted_iota(jnp.int32, (64, 64), 0)
    col = lax.broadcasted_iota(jnp.int32, (64, 64), 1)
    same = ((row >> 4) == ((col >> 2) & 3)) & (((row >> 2) & 3) == (col >> 4))
    return (same & ((row & 3) == (col & 3))).astype(BF16)


def pick(order, rows):
    return jnp.dot(order, rows, preferred_element_type=F32).astype(BF16)


def attend_kernel(length, query, cos, sin, krot, vnew, keys, values, out):
    heads = query.shape[1] // 256
    rows = query.shape[0]
    c = cos[...]
    s = sin[...]
    parts = []
    for h in range(heads):
        q = query[:, h * 256 : (h + 1) * 256].astype(F32)
        a = q[:, :128]
        b = q[:, 128:]
        parts.append(jnp.concatenate([a * c - b * s, a * s + b * c], axis=1))
    q = jnp.concatenate(parts, axis=0) * (1.0 / 16.0)
    n = heads * rows
    q0 = q.astype(BF16)
    rest = q - q0.astype(F32)
    q1 = rest.astype(BF16)
    q2 = (rest - q1.astype(F32)).astype(BF16)
    dims = (((1,), (1,)), ((), ()))
    k = keys[0]
    old = (
        lax.dot_general(q2, k, dims, preferred_element_type=F32)
        + lax.dot_general(q1, k, dims, preferred_element_type=F32)
    ) + lax.dot_general(q0, k, dims, preferred_element_type=F32)
    new = lax.dot_general(
        q, krot[...], dims, precision=lax.Precision.HIGHEST, preferred_element_type=F32
    )
    slot = lax.broadcasted_iota(jnp.int32, old.shape, 1)
    old = jnp.where(slot < length[0], old, -jnp.inf)
    step = lax.broadcasted_iota(jnp.int32, new.shape, 0) & 3
    place = lax.broadcasted_iota(jnp.int32, new.shape, 1)
    new = jnp.where(place <= step, new, -jnp.inf)
    top = jnp.maximum(jnp.max(old, axis=1, keepdims=True), jnp.max(new, axis=1, keepdims=True))
    old = jnp.exp(old - top)
    new = jnp.exp(new - top)
    total = jnp.sum(old, axis=1, keepdims=True) + jnp.sum(new, axis=1, keepdims=True)
    old = (old / total).astype(BF16)
    new = (new / total).astype(BF16)
    mixed = jnp.dot(old, values[0], preferred_element_type=F32) + jnp.dot(
        new, vnew[...], preferred_element_type=F32
    )
    mixed = mixed.astype(BF16)
    for h in range(heads):
        out[:, h * 256 : (h + 1) * 256] = mixed[h * rows : (h + 1) * rows]


def attend(query, cos, sin, krot, vnew, keys, values, length):
    spec = pl.BlockSpec(memory_space=pltpu.VMEM)
    return pl.pallas_call(
        attend_kernel,
        out_shape=jax.ShapeDtypeStruct(query.shape, BF16),
        in_specs=[pl.BlockSpec(memory_space=pltpu.SMEM)] + [spec] * 7,
        out_specs=spec,
        compiler_params=pltpu.CompilerParams(vmem_limit_bytes=32 * 1024 * 1024),
        cost_estimate=pl.CostEstimate(
            flops=2_000_000_000, bytes_accessed=2_400_000, transcendentals=400_000
        ),
        name="attend",
    )(length, query, cos, sin, krot, vnew, keys, values)


def tie(a, b):
    return lax.optimization_barrier((a, b))


def step_y(a, first):
    if first == 1:
        a = a.reshape(a.shape[0], 2, 2, *a.shape[2:])
        return a[:, :, 0], swap(a[:, :, 1].astype(BF16), "y", 1)
    return a[:, :2], swap(a[:, 2:].astype(BF16), "y", 3)


def scatter_y(a, first):
    a, got = step_y(a, first)
    a = a + got.astype(F32)
    got = swap(a[:, 1].astype(BF16), "y", 4 - first)
    return a[:, 0] + got.astype(F32)


def scatter_zh(a):
    got = swap(a[:, 1].astype(BF16), "zh", 1)
    return a[:, 0] + got.astype(F32)


def exchange_x(blocks):
    got = swap(jnp.stack([blocks[1], blocks[3]]), "x", 1)
    far = swap(jnp.stack([blocks[2], got[1]]), "x", 3)
    return jnp.concatenate([blocks[0], got[0], far[0], far[1]], axis=0)


def exchange_z(blocks):
    got = swap(jnp.stack([blocks[1], blocks[3]]), "zl", 1)
    far = swap(jnp.stack([blocks[2], got[1]]), "zl", 2)
    return jnp.concatenate([blocks[0], got[0], far[0], far[1]], axis=0)


def both(a, axis, mask):
    return jnp.concatenate([a, swap(a, axis, mask)], axis=0)


def body(
    tokens,
    ln_gain,
    w_gate,
    w_up,
    w_down,
    w_query,
    w_kv,
    w_out,
    cache_keys,
    cache_values,
    lengths,
    positions,
):
    width = tokens.shape[2]
    total = width * 16
    me = lax.axis_index("zh") * 8 + lax.axis_index("y") * 2 + lax.axis_index("c")
    own = tokens.reshape(64, width)
    order = row_order(me)
    turn = pair_order()
    gain = ln_gain.astype(F32)[None, :]

    near = jnp.concatenate([own] + [swap(own, "zl", m) for m in (1, 2, 3)], axis=0)
    vals = own.astype(F32)
    stat = jnp.stack([jnp.sum(vals, axis=1), jnp.sum(vals * vals, axis=1)])
    stat = stat + swap(stat, "c", 1)
    stat = stat + swap(stat, "y", 1)
    stat = stat + swap(stat, "y", 3)
    stat = stat + swap(stat, "zh", 1)

    n0 = pick(order, near)
    rows_a, rows_b = n0[:128], n0[128:]
    pair_a = both(rows_a, "x", 1)
    pair_b = both(rows_b, "x", 3)
    (pair_a, pair_b), stat = tie((pair_a, pair_b), stat)

    stat = both(both(stat[None], "zl", 1), "zl", 2)
    stat = jnp.concatenate(list(stat), axis=1)
    center = stat[0] / total
    stat = jnp.stack([center, lax.rsqrt(stat[1] / total - center * center + 1e-05)])
    stat = lax.dot_general(
        stat,
        order.astype(F32),
        (((1,), (1,)), ((), ())),
        precision=lax.Precision.HIGHEST,
        preferred_element_type=F32,
    )
    stats = both(both(stat[None], "x", 1), "x", 3)

    rows_a = both(pair_a, "x", 3)
    rows_b = both(pair_b, "x", 1)
    rows_b = rows_b.reshape(4, 128, width)
    rows_b = jnp.stack([rows_b[0], rows_b[2], rows_b[1], rows_b[3]]).reshape(512, width)

    def norm(rows, s):
        mid = jnp.concatenate([s[i, 0] for i in range(4)])[:, None]
        mul = jnp.concatenate([s[i, 1] for i in range(4)])[:, None]
        return ((rows.astype(F32) - mid) * mul * gain).astype(BF16)

    rows_a = norm(rows_a, stats[:, :, :128])
    rows_b = norm(rows_b, stats[:, :, 128:])
    rows_a, rows_b = tie(rows_a, rows_b)

    def away(*ws):
        parts = [jnp.dot(rows_b, w, preferred_element_type=F32).astype(BF16) for w in ws]
        return jnp.concatenate(parts, axis=1)

    def add(got, *ws):
        kept = [jnp.dot(rows_a, w, preferred_element_type=F32) for w in ws]
        part = jnp.concatenate(kept, axis=1) + got.astype(F32)
        return part.reshape(4, 4, 2, 16, part.shape[1])

    def fresh_part(rows):
        part = jnp.dot(rows, w_kv, preferred_element_type=F32)
        return jnp.concatenate([part[:, i * 128 : (i + 1) * 128] for i in range(4)], axis=0)

    q_away = jnp.concatenate([away(w_query), fresh_part(rows_b[:128]).astype(BF16)], axis=1)
    q_got = swap(q_away, "c", 1)
    gu_away = away(w_gate, w_up)
    q_got, gu_away = tie(q_got, gu_away)
    width_q = w_query.shape[1]
    q = add(q_got[:, :width_q], w_query)
    kv = fresh_part(rows_a[:128]) + q_got[:, width_q:].astype(F32)
    q = jnp.concatenate([q, kv.reshape(4, 4, 2, 16, 128)], axis=-1)
    gu = add(swap(gu_away, "c", 1), w_gate, w_up)
    half = width_q // 2
    ff = w_gate.shape[1]
    q_a, a_sent = step_y(q[..., :half], 1)
    q_b, b_sent = step_y(q[..., half:], 3)
    a_sent, gu = tie(a_sent, gu)
    q_a = q_a + a_sent.astype(F32)
    q_b = q_b + b_sent.astype(F32)
    q_a = q_a[:, 0] + swap(q_a[:, 1].astype(BF16), "y", 3).astype(F32)
    q_b = q_b[:, 0] + swap(q_b[:, 1].astype(BF16), "y", 1).astype(F32)
    query = scatter_zh(jnp.concatenate([q_a, q_b], axis=-1))
    fresh = jnp.concatenate([query[i, :4, width_q:] for i in range(4)], axis=1).astype(BF16)
    query = query[..., :width_q].astype(BF16)
    gu, gu_sent = step_y(gu, 1)

    angle = (positions + jnp.arange(4)).astype(F32)[:, None] * (
        10000.0 ** (-(jnp.arange(128).astype(F32) * 2.0 / 256))
    )
    cos, sin = jnp.cos(angle), jnp.sin(angle)
    ka, kc = fresh[:, :128].astype(F32), fresh[:, 128:256].astype(F32)
    krot = jnp.concatenate([ka * cos - kc * sin, ka * sin + kc * cos], axis=1)
    krot = jnp.pad(krot, ((0, 124), (0, 0)))
    vnew = jnp.pad(fresh[:, 256:], ((0, 124), (0, 0)))
    cos64, sin64 = jnp.tile(cos, (16, 1)), jnp.tile(sin, (16, 1))

    q = pick(turn, exchange_x(query)).reshape(4, 16, -1)
    q, gu_sent = tie(q, gu_sent)
    gu = gu + gu_sent.astype(F32)
    gu_sent = swap(gu[:, 1].astype(BF16), "y", 3)
    q = exchange_z(q)
    q, gu_sent = tie(q, gu_sent)
    ctx = attend(q, cos64, sin64, krot, vnew, cache_keys, cache_values, lengths)
    gu = gu[:, 0] + gu_sent.astype(F32)
    gu_sent = swap(gu[:, 1].astype(BF16), "zh", 1)
    ctx = pick(turn, exchange_z(ctx.reshape(4, 16, -1))).reshape(4, 16, -1)
    ctx, gu_sent = tie(ctx, gu_sent)
    gu = (gu[:, 0] + gu_sent.astype(F32)).reshape(64, -1)
    hidden = (jax.nn.silu(gu[:, :ff]) * gu[:, ff:]).astype(BF16)
    ctx = exchange_x(ctx)

    mine = jnp.concatenate([ctx, hidden], axis=1)[None]
    other = swap(mine, "zh", 1)
    mine = both(both(mine, "y", 1), "y", 3)
    other = both(both(other, "y", 1), "y", 3)
    here = jnp.stack([mine, other], axis=1).reshape(512, -1)
    there = swap(here, "c", 1)

    def product(r):
        split = w_out.shape[0]
        o = jnp.dot(r[:, :split], w_out, preferred_element_type=F32)
        o = o + jnp.dot(r[:, split:], w_down, preferred_element_type=F32)
        return o.reshape(8, 4, 16, width)

    ra = product(here)
    there, ra = tie(there, ra)
    rb = product(there)
    ra = ra.reshape(8, 2, 2, 16, width)
    ra = ra[:, :, 0] + swap(ra[:, :, 1].astype(BF16), "x", 1).astype(F32)
    rb = rb[:, :2] + swap(rb[:, 2:].astype(BF16), "x", 3).astype(F32)
    ra = ra[:, 0] + swap(ra[:, 1].astype(BF16), "x", 3).astype(F32)
    rb = rb[:, 0] + swap(rb[:, 1].astype(BF16), "x", 1).astype(F32)
    r = jnp.concatenate([ra.reshape(128, width), rb.reshape(128, width)], axis=0).astype(BF16)
    r = lax.dot_general(order, r, (((0,), (0,)), ((), ())), preferred_element_type=F32)
    r = r.astype(BF16).reshape(4, 64, width)
    mixed = r[0].astype(F32)
    for m in (1, 2, 3):
        mixed = mixed + swap(r[m], "zl", m).astype(F32)
    return (vals + mixed).astype(BF16).reshape(tokens.shape)


def solution(mesh):
    fine = Mesh(mesh.devices.reshape(4, 4, 2, 4, 2), ("zl", "x", "zh", "y", "c"))
    ffn = ("zl", "x")
    emb = ("zh", "y", "c")
    every = ffn + emb
    placed = (
        P(ffn, None, emb),
        P(emb),
        P(emb, ffn),
        P(emb, ffn),
        P(ffn, emb),
        P(emb, ffn),
        P(emb, None),
        P(ffn, emb),
        P(every, None, None),
        P(every, None, None),
        P(every),
        P(every),
    )
    return jax.shard_map(
        body, mesh=fine, in_specs=placed, out_specs=P(ffn, None, emb), check_vma=False
    )
```

```python
import jax
import jax.numpy as jnp
from jax import lax
from jax.experimental import pallas as pl
from jax.experimental.pallas import tpu as pltpu
from jax.sharding import Mesh, PartitionSpec as P

F32 = jnp.float32
BF16 = jnp.bfloat16
SIZES = {"zl": 4, "x": 4, "zh": 2, "y": 4, "c": 2}


def swap(a, axis, mask):
    return lax.ppermute(a, axis, [(i, i ^ mask) for i in range(SIZES[axis])])


def row_order(me):
    row = lax.broadcasted_iota(jnp.int32, (256, 256), 0)
    col = lax.broadcasted_iota(jnp.int32, (256, 256), 1)
    code = (row >> 5) & 3
    k = ((row >> 4) & 1) * 8 + (code ^ (code >> 1)) * 2 + (row >> 7)
    same = ((row >> 2) & 3) == (col >> 6)
    same = same & ((row & 3) == (col & 3))
    return (same & (((col >> 2) & 15) == (k ^ me))).astype(BF16)


def pair_order():
    row = lax.broadcasted_iota(jnp.int32, (64, 64), 0)
    col = lax.broadcasted_iota(jnp.int32, (64, 64), 1)
    same = ((row >> 4) == ((col >> 2) & 3)) & (((row >> 2) & 3) == (col >> 4))
    return (same & ((row & 3) == (col & 3))).astype(BF16)


def pick(order, rows):
    return jnp.dot(order, rows, preferred_element_type=F32).astype(BF16)


def attend_kernel(length, query, cos, sin, krot, vnew, keys, values, out):
    heads = query.shape[1] // 256
    rows = query.shape[0]
    c = cos[...]
    s = sin[...]
    parts = []
    for h in range(heads):
        q = query[:, h * 256 : (h + 1) * 256].astype(F32)
        a = q[:, :128]
        b = q[:, 128:]
        parts.append(jnp.concatenate([a * c - b * s, a * s + b * c], axis=1))
    q = jnp.concatenate(parts, axis=0) * (1.0 / 16.0)
    n = heads * rows
    q0 = q.astype(BF16)
    rest = q - q0.astype(F32)
    q1 = rest.astype(BF16)
    q2 = (rest - q1.astype(F32)).astype(BF16)
    dims = (((1,), (1,)), ((), ()))
    k = keys[0]
    old = (
        lax.dot_general(q2, k, dims, preferred_element_type=F32)
        + lax.dot_general(q1, k, dims, preferred_element_type=F32)
    ) + lax.dot_general(q0, k, dims, preferred_element_type=F32)
    new = lax.dot_general(
        q, krot[...], dims, precision=lax.Precision.HIGHEST, preferred_element_type=F32
    )
    slot = lax.broadcasted_iota(jnp.int32, old.shape, 1)
    old = jnp.where(slot < length[0], old, -jnp.inf)
    step = lax.broadcasted_iota(jnp.int32, new.shape, 0) & 3
    place = lax.broadcasted_iota(jnp.int32, new.shape, 1)
    new = jnp.where(place <= step, new, -jnp.inf)
    top = jnp.maximum(jnp.max(old, axis=1, keepdims=True), jnp.max(new, axis=1, keepdims=True))
    old = jnp.exp(old - top)
    new = jnp.exp(new - top)
    total = jnp.sum(old, axis=1, keepdims=True) + jnp.sum(new, axis=1, keepdims=True)
    old = (old / total).astype(BF16)
    new = (new / total).astype(BF16)
    mixed = jnp.dot(old, values[0], preferred_element_type=F32) + jnp.dot(
        new, vnew[...], preferred_element_type=F32
    )
    mixed = mixed.astype(BF16)
    for h in range(heads):
        out[:, h * 256 : (h + 1) * 256] = mixed[h * rows : (h + 1) * rows]


def attend(query, cos, sin, krot, vnew, keys, values, length):
    spec = pl.BlockSpec(memory_space=pltpu.VMEM)
    return pl.pallas_call(
        attend_kernel,
        out_shape=jax.ShapeDtypeStruct(query.shape, BF16),
        in_specs=[pl.BlockSpec(memory_space=pltpu.SMEM)] + [spec] * 7,
        out_specs=spec,
        compiler_params=pltpu.CompilerParams(vmem_limit_bytes=32 * 1024 * 1024),
        cost_estimate=pl.CostEstimate(
            flops=2_000_000_000, bytes_accessed=2_400_000, transcendentals=400_000
        ),
        name="attend",
    )(length, query, cos, sin, krot, vnew, keys, values)


def tie(a, b):
    return lax.optimization_barrier((a, b))


def step_y(a, first):
    if first == 1:
        a = a.reshape(a.shape[0], 2, 2, *a.shape[2:])
        return a[:, :, 0], swap(a[:, :, 1].astype(BF16), "y", 1)
    return a[:, :2], swap(a[:, 2:].astype(BF16), "y", 3)


def scatter_y(a, first):
    a, got = step_y(a, first)
    a = a + got.astype(F32)
    got = swap(a[:, 1].astype(BF16), "y", 4 - first)
    return a[:, 0] + got.astype(F32)


def scatter_zh(a):
    got = swap(a[:, 1].astype(BF16), "zh", 1)
    return a[:, 0] + got.astype(F32)


def exchange_x(blocks):
    got = swap(jnp.stack([blocks[1], blocks[3]]), "x", 1)
    far = swap(jnp.stack([blocks[2], got[1]]), "x", 3)
    return jnp.concatenate([blocks[0], got[0], far[0], far[1]], axis=0)


def exchange_z(blocks):
    got = swap(jnp.stack([blocks[1], blocks[3]]), "zl", 1)
    far = swap(jnp.stack([blocks[2], got[1]]), "zl", 2)
    return jnp.concatenate([blocks[0], got[0], far[0], far[1]], axis=0)


def both(a, axis, mask):
    return jnp.concatenate([a, swap(a, axis, mask)], axis=0)


def body(
    tokens,
    ln_gain,
    w_gate,
    w_up,
    w_down,
    w_query,
    w_kv,
    w_out,
    cache_keys,
    cache_values,
    lengths,
    positions,
):
    width = tokens.shape[2]
    total = width * 16
    me = lax.axis_index("zh") * 8 + lax.axis_index("y") * 2 + lax.axis_index("c")
    own = tokens.reshape(64, width)
    order = row_order(me)
    turn = pair_order()
    gain = ln_gain.astype(F32)[None, :]

    near = jnp.concatenate([own] + [swap(own, "zl", m) for m in (1, 2, 3)], axis=0)
    vals = own.astype(F32)
    stat = jnp.stack([jnp.sum(vals, axis=1), jnp.sum(vals * vals, axis=1)])
    stat = stat + swap(stat, "c", 1)
    stat = stat + swap(stat, "y", 1)
    stat = stat + swap(stat, "y", 3)
    stat = stat + swap(stat, "zh", 1)

    n0 = pick(order, near)
    rows_a, rows_b = n0[:128], n0[128:]
    pair_a = both(rows_a, "x", 1)
    pair_b = both(rows_b, "x", 3)
    (pair_a, pair_b), stat = tie((pair_a, pair_b), stat)

    stat = both(both(stat[None], "zl", 1), "zl", 2)
    stat = jnp.concatenate(list(stat), axis=1)
    center = stat[0] / total
    stat = jnp.stack([center, lax.rsqrt(stat[1] / total - center * center + 1e-05)])
    stat = lax.dot_general(
        stat,
        order.astype(F32),
        (((1,), (1,)), ((), ())),
        precision=lax.Precision.HIGHEST,
        preferred_element_type=F32,
    )
    stats = both(both(stat[None], "x", 1), "x", 3)

    rows_a = both(pair_a, "x", 3)
    rows_b = both(pair_b, "x", 1)
    rows_b = rows_b.reshape(4, 128, width)
    rows_b = jnp.stack([rows_b[0], rows_b[2], rows_b[1], rows_b[3]]).reshape(512, width)

    def norm(rows, s):
        mid = jnp.concatenate([s[i, 0] for i in range(4)])[:, None]
        mul = jnp.concatenate([s[i, 1] for i in range(4)])[:, None]
        return ((rows.astype(F32) - mid) * mul * gain).astype(BF16)

    rows_a = norm(rows_a, stats[:, :, :128])
    rows_b = norm(rows_b, stats[:, :, 128:])
    rows_a, rows_b = tie(rows_a, rows_b)

    def away(*ws):
        parts = [jnp.dot(rows_b, w, preferred_element_type=F32).astype(BF16) for w in ws]
        return jnp.concatenate(parts, axis=1)

    def add(got, *ws):
        kept = [jnp.dot(rows_a, w, preferred_element_type=F32) for w in ws]
        part = jnp.concatenate(kept, axis=1) + got.astype(F32)
        return part.reshape(4, 4, 2, 16, part.shape[1])

    def fresh_part(rows):
        part = jnp.dot(rows, w_kv, preferred_element_type=F32)
        return jnp.concatenate([part[:, i * 128 : (i + 1) * 128] for i in range(4)], axis=0)

    q_away = jnp.concatenate([away(w_query), fresh_part(rows_b[:128]).astype(BF16)], axis=1)
    q_got = swap(q_away, "c", 1)
    gu_away = away(w_gate, w_up)
    q_got, gu_away = tie(q_got, gu_away)
    width_q = w_query.shape[1]
    q = add(q_got[:, :width_q], w_query)
    kv = fresh_part(rows_a[:128]) + q_got[:, width_q:].astype(F32)
    q = jnp.concatenate([q, kv.reshape(4, 4, 2, 16, 128)], axis=-1)
    gu = add(swap(gu_away, "c", 1), w_gate, w_up)
    half = width_q // 2
    ff = w_gate.shape[1]
    q_a, a_sent = step_y(q[..., :half], 1)
    q_b, b_sent = step_y(q[..., half:], 3)
    a_sent, gu = tie(a_sent, gu)
    q_a = q_a + a_sent.astype(F32)
    q_b = q_b + b_sent.astype(F32)
    q_a = q_a[:, 0] + swap(q_a[:, 1].astype(BF16), "y", 3).astype(F32)
    q_b = q_b[:, 0] + swap(q_b[:, 1].astype(BF16), "y", 1).astype(F32)
    query = scatter_zh(jnp.concatenate([q_a, q_b], axis=-1))
    fresh = jnp.concatenate([query[i, :4, width_q:] for i in range(4)], axis=1).astype(BF16)
    query = query[..., :width_q].astype(BF16)
    gu, gu_sent = step_y(gu, 1)

    angle = (positions + jnp.arange(4)).astype(F32)[:, None] * (
        10000.0 ** (-(jnp.arange(128).astype(F32) * 2.0 / 256))
    )
    cos, sin = jnp.cos(angle), jnp.sin(angle)
    ka, kc = fresh[:, :128].astype(F32), fresh[:, 128:256].astype(F32)
    krot = jnp.concatenate([ka * cos - kc * sin, ka * sin + kc * cos], axis=1)
    krot = jnp.pad(krot, ((0, 124), (0, 0)))
    vnew = jnp.pad(fresh[:, 256:], ((0, 124), (0, 0)))
    cos64, sin64 = jnp.tile(cos, (16, 1)), jnp.tile(sin, (16, 1))

    q = pick(turn, exchange_x(query)).reshape(4, 16, -1)
    q, gu_sent = tie(q, gu_sent)
    gu = gu + gu_sent.astype(F32)
    gu_sent = swap(gu[:, 1].astype(BF16), "y", 3)
    q = exchange_z(q)
    ctx = attend(q, cos64, sin64, krot, vnew, cache_keys, cache_values, lengths)
    gu = gu[:, 0] + gu_sent.astype(F32)
    gu_sent = swap(gu[:, 1].astype(BF16), "zh", 1)
    ctx = pick(turn, exchange_z(ctx.reshape(4, 16, -1))).reshape(4, 16, -1)
    ctx, gu_sent = tie(ctx, gu_sent)
    gu = (gu[:, 0] + gu_sent.astype(F32)).reshape(64, -1)
    hidden = (jax.nn.silu(gu[:, :ff]) * gu[:, ff:]).astype(BF16)
    ctx = exchange_x(ctx)

    mine = jnp.concatenate([ctx, hidden], axis=1)[None]
    other = swap(mine, "zh", 1)
    mine = both(both(mine, "y", 1), "y", 3)
    other = both(both(other, "y", 1), "y", 3)
    here = jnp.stack([mine, other], axis=1).reshape(512, -1)
    there = swap(here, "c", 1)

    def product(r):
        split = w_out.shape[0]
        o = jnp.dot(r[:, :split], w_out, preferred_element_type=F32)
        o = o + jnp.dot(r[:, split:], w_down, preferred_element_type=F32)
        return o.reshape(8, 4, 16, width)

    ra = product(here)
    there, ra = tie(there, ra)
    rb = product(there)
    ra = ra.reshape(8, 2, 2, 16, width)
    ra = ra[:, :, 0] + swap(ra[:, :, 1].astype(BF16), "x", 1).astype(F32)
    rb = rb[:, :2] + swap(rb[:, 2:].astype(BF16), "x", 3).astype(F32)
    ra = ra[:, 0] + swap(ra[:, 1].astype(BF16), "x", 3).astype(F32)
    rb = rb[:, 0] + swap(rb[:, 1].astype(BF16), "x", 1).astype(F32)
    r = jnp.concatenate([ra.reshape(128, width), rb.reshape(128, width)], axis=0).astype(BF16)
    r = lax.dot_general(order, r, (((0,), (0,)), ((), ())), preferred_element_type=F32)
    r = r.astype(BF16).reshape(4, 64, width)
    mixed = r[0].astype(F32)
    for m in (1, 2, 3):
        mixed = mixed + swap(r[m], "zl", m).astype(F32)
    return (vals + mixed).astype(BF16).reshape(tokens.shape)


def solution(mesh):
    fine = Mesh(mesh.devices.reshape(4, 4, 2, 4, 2), ("zl", "x", "zh", "y", "c"))
    ffn = ("zl", "x")
    emb = ("zh", "y", "c")
    every = ffn + emb
    placed = (
        P(ffn, None, emb),
        P(emb),
        P(emb, ffn),
        P(emb, ffn),
        P(ffn, emb),
        P(emb, ffn),
        P(emb, None),
        P(ffn, emb),
        P(every, None, None),
        P(every, None, None),
        P(every),
        P(every),
    )
    return jax.shard_map(
        body, mesh=fine, in_specs=placed, out_specs=P(ffn, None, emb), check_vma=False
    )
```
